256 devices in a mesh: attn: 2 (over y_hi), wa: 4 (over x), ha: 32 (over z, y_lo, core).
Axes of the slice: x: 4, y: 4 (y_hi: 2, y_lo: 2; y = y_hi * 2 + y_lo), z: 8, core: 2. Of those that a mesh axis runs over, the one named last changes fastest.
Arguments:
- tokens: bfloat16 [1024, 16384], P(('attn', 'ha'), 'wa'), may hold values from -6 to 6
- counts: int32 [4], replicated, may hold values from 128 to 256, as said below
- starts: int32 [4], replicated, may hold values from 0 to 128, as said below
- gate_weight: bfloat16 [16384, 32768], P('wa', ('attn', 'ha')), may hold values from -0.046875 to 0.046875
- up_weight: bfloat16 [16384, 32768], P('wa', ('attn', 'ha')), may hold values from -0.046875 to 0.046875
- down_weight: bfloat16 [32768, 16384], P(('attn', 'ha'), 'wa'), may hold values from -0.03125 to 0.03125
Outputs:
- returned: bfloat16 [1024, 16384], P(('attn', 'ha'), 'wa')
The draws below stay inside these ranges and needn't reach their ends.
Inputs may be any that keep to these rules, and one draw needn't show every extreme that they name: counts[g] lies between 128 and 256; some group has exactly 256, some other group exactly 128. starts[g] + counts[g] <= 256.
All inputs are finite; a program needn't handle non-finite values.
Results may differ from the reference program's by a relative error of at most 0.0049.
Values may be sent and summed in bfloat16 or wider, within the bound.
No kernel may reach another device: no remote copies, remote signals or barrier semaphores. Data moves between devices by JAX's collectives and lax.ppermute only.
A program may use at most 128 MiB of HBM per device.

```python
import jax
import jax.numpy as jnp
from jax import lax

D = 16384
FF = 32768
GROUPS = 4
CAP = 256
ROWS = 1024


def ragged_rows(key):
    first, second, third, fourth = jax.random.split(key, 4)
    counts = jax.random.randint(first, (GROUPS,), CAP // 2, CAP + 1)
    fullest = jax.random.randint(second, (), 0, GROUPS)
    emptiest = (fullest + 1 + jax.random.randint(fourth, (), 0, GROUPS - 1)) % GROUPS
    group_ids = jnp.arange(GROUPS)
    counts = jnp.where(group_ids == fullest, CAP, counts)
    counts = jnp.where(group_ids == emptiest, CAP // 2, counts).astype(jnp.int32)
    starts = jax.random.randint(third, (GROUPS,), 0, CAP - counts + 1)
    starts = jnp.where(group_ids == emptiest, CAP - CAP // 2, starts).astype(jnp.int32)
    return (counts, starts)


def draw_counts(key, part):
    return ragged_rows(key)[0]


def draw_starts(key, part):
    return ragged_rows(key)[1]


def steps_of(stream_key, extent, cuts, low, top_value):
    def one(dim, shards_of):
        steps = jax.random.uniform(jax.random.fold_in(jax.random.fold_in(stream_key, 6), dim), (shards_of,), jnp.float32, low / len(cuts), top_value / len(cuts))
        return jnp.repeat(jnp.exp(steps), extent[dim] // shards_of).reshape((-1,) + (1,) * (len(extent) - dim - 1))

    factor_of = one(*cuts[0])
    for cut in cuts[1:]:
        factor_of = factor_of * one(*cut)
    return factor_of


def bell_draw(rng, dims, width, most, cuts=(), kind=jnp.bfloat16):
    array = jax.random.normal(rng, dims, jnp.float32) * width
    if len(cuts) > 0:
        array = steps_of(rng, dims, cuts, -0.22, 0.18) * array
    return jnp.clip(array, min=-most, max=most).astype(kind)


def setup_inputs(seed: int = 0) -> dict:
    keys = jax.random.split(jax.random.key(seed), 7)
    tokens = bell_draw(keys[0], (ROWS, D), 1.0, 6.0, ((0, 64), (1, 4)))
    counts = draw_counts(jax.random.fold_in(keys[6], 71), 0)
    starts = draw_starts(jax.random.fold_in(keys[6], 71), 0)
    gate_weight = bell_draw(keys[3], (D, FF), D ** -0.5, 0.046875, ((0, 4), (1, 64)))
    up_weight = bell_draw(keys[4], (D, FF), D ** -0.5, 0.046875, ((0, 4), (1, 64)))
    down_weight = bell_draw(keys[5], (FF, D), FF ** -0.5, 0.03125, ((0, 64), (1, 4)))
    return {"tokens": tokens, "counts": counts, "starts": starts, "gate_weight": gate_weight, "up_weight": up_weight, "down_weight": down_weight}


def reference(tokens, counts, starts, gate_weight, up_weight, down_weight):
    block = FF // 8

    def one_block(index):
        first = (index * block).astype(jnp.int32)
        gate_part = lax.dynamic_slice_in_dim(gate_weight, first, block, 1)
        up_part = lax.dynamic_slice_in_dim(up_weight, first, block, 1)
        down_part = lax.dynamic_slice_in_dim(down_weight, first, block, 0)
        gate = jnp.dot(tokens, gate_part, preferred_element_type=jnp.float32)
        up_val = jnp.dot(tokens, up_part, preferred_element_type=jnp.float32)
        hidden = (jax.nn.silu(gate) * up_val).astype(jnp.bfloat16)
        return jnp.dot(hidden, down_part, preferred_element_type=jnp.float32)

    total = jnp.zeros((ROWS, D), jnp.float32)
    for index in range(8):
        total = total + one_block(jnp.int32(index))
    row_ids = jnp.arange(ROWS, dtype=jnp.int32)
    group = row_ids // CAP
    slot = row_ids % CAP
    start_row = starts[group]
    live = (slot >= start_row) & (slot < start_row + counts[group])
    return jnp.where(live[:, None], total, 0.0).astype(jnp.bfloat16)
```

```python
import jax
import jax.numpy as jnp
from jax import lax
from jax.sharding import Mesh, PartitionSpec as P

GROUPS = 4
CAP = 256
Y = ("attn", "yl")
SIZE = {"z": 8, Y: 4, "wa": 4, "core": 2}
BF16 = jnp.bfloat16
F32 = jnp.float32


def shift(value, axis, by):
    size = SIZE[axis]
    return lax.ppermute(value, axis, [(i, (i + by) % size) for i in range(size)])


def dot(a, b):
    return jnp.dot(a, b, preferred_element_type=F32)


def live_rows(counts, starts, local_rows):
    first_row = lax.axis_index(("attn", "z", "yl", "core")) * local_rows
    row_ids = first_row + jnp.arange(local_rows, dtype=jnp.int32)
    group = row_ids // CAP
    slot = row_ids % CAP
    onehot = (group[:, None] == jnp.arange(GROUPS, dtype=jnp.int32)[None, :]).astype(jnp.int32)
    start_row = jnp.sum(onehot * starts[None, :], axis=1)
    live_count = jnp.sum(onehot * counts[None, :], axis=1)
    return (slot >= start_row) & (slot < start_row + live_count)


def on_device(tokens, counts, starts, gate_weight, up_weight, down_weight):
    local_rows = tokens.shape[0]
    width = gate_weight.shape[1]
    with jax.named_scope("swap_weights"):
        gate_other = shift(gate_weight, "core", 1)
        up_other = shift(up_weight, "core", 1)
        down_other = shift(down_weight, "core", 1)
    with jax.named_scope("gather_z"):
        by_z = {0: tokens}
        ahead = back = tokens
        for step in range(1, 5):
            ahead = shift(ahead, "z", 1)
            by_z[8 - step] = ahead
            if step < 4:
                back = shift(back, "z", -1)
                by_z[step] = back
        mine = jnp.concatenate([by_z[i] for i in range(8)], axis=0)
    with jax.named_scope("gather_y"):
        by_y = [mine, shift(mine, Y, -1), shift(mine, Y, 2), shift(mine, Y, 1)]
    with jax.named_scope("gate_up"):
        parts = []
        for rows in by_y:
            parts.append(
                jnp.concatenate(
                    [dot(rows, w).astype(BF16) for w in (gate_weight, gate_other, up_weight, up_other)], axis=1
                )
            )
    with jax.named_scope("sum_x"):
        pieces = lax.all_to_all(jnp.concatenate(parts, axis=0), "wa", 0, 0, tiled=True)
        pieces = pieces.reshape(4, -1, 4 * width).astype(F32)
        total = pieces[0] + pieces[1] + pieces[2] + pieces[3]
        hidden = (jax.nn.silu(total[:, : 2 * width]) * total[:, 2 * width :]).astype(BF16)
    with jax.named_scope("gather_x"):
        by_x = [hidden, shift(hidden, "wa", -1), shift(hidden, "wa", 2), shift(hidden, "wa", 1)]
        piece_rows = hidden.shape[0]
        twice = jnp.concatenate(by_x + by_x, axis=0)
        first = lax.rem(4 - lax.axis_index("wa"), 4) * piece_rows
        hidden_all = lax.dynamic_slice_in_dim(twice, first, 4 * piece_rows, 0)
    with jax.named_scope("down"):
        outs = []
        for i in range(4):
            rows = hidden_all[i * piece_rows : (i + 1) * piece_rows]
            outs.append(dot(rows[:, :width], down_weight) + dot(rows[:, width:], down_other))
    with jax.named_scope("sum_y"):
        total = outs[0]
        for i, by in ((1, 1), (3, -1), (2, 2)):
            total = total + shift(outs[i].astype(BF16), Y, by).astype(F32)
    with jax.named_scope("sum_z"):
        result = total[:local_rows]
        for i in (4, 3, 5, 2, 6, 1, 7):
            block = total[i * local_rows : (i + 1) * local_rows].astype(BF16)
            result = result + shift(block, "z", i if i <= 4 else i - 8).astype(F32)
    live = live_rows(counts, starts, local_rows)
    return jnp.where(live[:, None], result, 0.0).astype(BF16)


def solution(mesh):
    fine = Mesh(mesh.devices.reshape(2, 4, 8, 2, 2), ("attn", "wa", "z", "yl", "core"))
    rows = ("attn", "z", "yl", "core")
    placed = (P(rows, "wa"), P(), P(), P("wa", rows), P("wa", rows), P(rows, "wa"))
    return jax.shard_map(on_device, mesh=fine, in_specs=placed, out_specs=P(rows, "wa"), check_vma=False)
```

```python
import functools

import jax
import jax.numpy as jnp
from jax import lax
from jax.experimental import pallas as pl
from jax.experimental.pallas import tpu as pltpu
from jax.sharding import Mesh, PartitionSpec as P

GROUPS = 4
CAP = 256
Y = ("attn", "yl")
SIZE = {"z": 8, Y: 4, "wa": 4, "core": 2}
BF16 = jnp.bfloat16
F32 = jnp.float32
CHUNKS = ((0, 1, 7, 4), (2, 3, 6, 5))
DOWN_TILE = 2048
VMEM = 58 * 1024 * 1024


def shift(value, axis, by):
    size = SIZE[axis]
    return lax.ppermute(value, axis, [(i, (i + by) % size) for i in range(size)])


def dot(a, b):
    return jnp.dot(a, b, preferred_element_type=F32)


def gate_up_kernel(x_ref, p0, p1, p2, p3, w0, w1, w2, w3, o0, o1, o2, o3, lhs, held, sems, row_sems):
    rows = p0.shape[0]
    half = held.shape[1] // 2
    copies = [
        [
            pltpu.make_async_copy(
                w.at[pl.ds(part * half, half)], held.at[k, pl.ds(part * half, half)], sems.at[2 * k + part]
            )
            for part in range(2)
        ]
        for k, w in enumerate((w0, w1, w2, w3))
    ]
    into = []
    for j, p in enumerate((p0, p1, p2, p3)):
        place = pl.multiple_of(lax.rem(4 + j - x_ref[0], 4) * rows, rows)
        into.append(pltpu.make_async_copy(p, lhs.at[pl.ds(place, rows)], row_sems.at[j]))
        into[j].start()
    for copy in copies[0] + copies[1]:
        copy.start()
    for copy in into:
        copy.wait()
    for k in range(4):
        for copy in copies[k]:
            copy.wait()
        if k + 2 < 4:
            for copy in copies[k + 2]:
                copy.start()
        part = dot(lhs[...], held[k])
        for d, o in enumerate((o0, o1, o2, o3)):
            o[k] = part[d * rows : (d + 1) * rows].astype(o.dtype)


def gate_up(x, by_y, weights):
    rows, depth = by_y[0].shape
    width = weights[0].shape[1]
    whole = pl.BlockSpec(memory_space=pltpu.VMEM)
    return pl.pallas_call(
        gate_up_kernel,
        out_shape=[jax.ShapeDtypeStruct((4, rows, width), F32 if d == 0 else BF16) for d in range(4)],
        in_specs=[pl.BlockSpec(memory_space=pltpu.SMEM)] + [pl.BlockSpec(memory_space=pl.ANY)] * 8,
        out_specs=[whole] * 4,
        scratch_shapes=[
            pltpu.VMEM((4 * rows, depth), BF16),
            pltpu.VMEM((4, depth, width), BF16),
            pltpu.SemaphoreType.DMA((8,)),
            pltpu.SemaphoreType.DMA((4,)),
        ],
        compiler_params=pltpu.CompilerParams(vmem_limit_bytes=VMEM),
        cost_estimate=pl.CostEstimate(flops=1, bytes_accessed=1, transcendentals=0),
        name="gate_up",
    )(x, *by_y, *weights)


def down_kernel(x_ref, h0, h1, h2, h3, down, down_other, o0, o1, o2, o3, lhs):
    rows, width = h0.shape[1:]

    @pl.when(pl.program_id(0) == 0)
    def _():
        for d, h in enumerate((h0, h1, h2, h3)):
            place = pl.multiple_of(lax.rem(x_ref[0] + d, 4) * rows, rows)
            lhs[pl.ds(place, rows), :width] = h[0]
            lhs[pl.ds(place, rows), width:] = h[1]

    total = dot(lhs[...], jnp.concatenate([down[...], down_other[...]], axis=0))
    for j, o in enumerate((o0, o1, o2, o3)):
        o[...] = total[j * rows : (j + 1) * rows].astype(o.dtype)


def down_project(x, by_x, weights):
    _, rows, width = by_x[0].shape
    columns = weights[0].shape[1]
    out = pl.BlockSpec((rows, DOWN_TILE), lambda n, x_ref: (0, n))
    return pl.pallas_call(
        down_kernel,
        out_shape=[jax.ShapeDtypeStruct((rows, columns), F32 if j == 0 else BF16) for j in range(4)],
        grid_spec=pltpu.PrefetchScalarGridSpec(
            num_scalar_prefetch=1,
            grid=(columns // DOWN_TILE,),
            in_specs=[pl.BlockSpec((2, rows, width), lambda n, x_ref: (0, 0, 0))] * 4
            + [pl.BlockSpec((width, DOWN_TILE), lambda n, x_ref: (0, n))] * 2,
            out_specs=[out] * 4,
            scratch_shapes=[pltpu.VMEM((4 * rows, 2 * width), BF16)],
        ),
        compiler_params=pltpu.CompilerParams(vmem_limit_bytes=VMEM),
        cost_estimate=pl.CostEstimate(
            flops=2 * 4 * rows * 2 * width * columns, bytes_accessed=4 * width * columns, transcendentals=0
        ),
        name="down",
    )(x, *by_x, *weights)


def live_rows(counts, starts, local_rows):
    first_row = lax.axis_index(("attn", "z", "yl", "core")) * local_rows
    row_ids = first_row + jnp.arange(local_rows, dtype=jnp.int32)
    group = row_ids // CAP
    slot = row_ids % CAP
    onehot = (group[:, None] == jnp.arange(GROUPS, dtype=jnp.int32)[None, :]).astype(jnp.int32)
    start_row = jnp.sum(onehot * starts[None, :], axis=1)
    live_count = jnp.sum(onehot * counts[None, :], axis=1)
    return (slot >= start_row) & (slot < start_row + live_count)


def on_device(tokens, counts, starts, gate_weight, up_weight, down_weight):
    local_rows = tokens.shape[0]
    x = lax.axis_index("wa").astype(jnp.int32).reshape(1)
    with jax.named_scope("swap_weights"):
        gate_other = shift(gate_weight, "core", 1)
        up_other = shift(up_weight, "core", 1)
    with jax.named_scope("gather_z"):
        after = shift(tokens, "z", -1)
        before = shift(tokens, "z", 1)
        far = shift(tokens, "z", 4)
        after, before, far, gate_other, up_other = lax.optimization_barrier(
            (after, before, far, gate_other, up_other)
        )
        near = jnp.concatenate([tokens, after, before, far], axis=0)
        afters = shift(jnp.concatenate([tokens, after], axis=0), "z", -2)
        befores = shift(jnp.concatenate([tokens, before], axis=0), "z", 2)
        rest = jnp.concatenate([afters, befores], axis=0)
    with jax.named_scope("gather_y"):
        near_y, rest_y = [[m, shift(m, Y, -1), shift(m, Y, 2), shift(m, Y, 1)] for m in (near, rest)]

    def products(by_y):
        with jax.named_scope("gate_up"):
            return gate_up(x, by_y, (gate_weight, gate_other, up_weight, up_other))

    def exchange_x(parts):
        with jax.named_scope("sum_x"):
            return [parts[0], shift(parts[1], "wa", 1), shift(parts[3], "wa", -1), shift(parts[2], "wa", 2)]

    def activate(parts):
        with jax.named_scope("sum_x"):
            total = parts[0]
            for part in parts[1:]:
                total = total + part.astype(F32)
            return (jax.nn.silu(total[:2]) * total[2:]).astype(BF16)

    def gather_x(hidden):
        with jax.named_scope("gather_x"):
            return [hidden, shift(hidden, "wa", -1), shift(hidden, "wa", 2), shift(hidden, "wa", 1)]

    def sum_y(parts):
        with jax.named_scope("sum_y"):
            total = parts[0]
            for q, by in ((parts[1], 1), (parts[3], -1), (parts[2], 2)):
                total = total + shift(q, Y, by).astype(F32)
            return total

    parts = exchange_x(products(near_y))
    tied = lax.optimization_barrier((*parts, *rest_y))
    hidden, down_tied, *rest_y = lax.optimization_barrier((activate(tied[:4]), down_weight, *tied[4:]))
    with jax.named_scope("swap_down"):
        down_other = shift(down_tied, "core", 1)
    by_x = gather_x(hidden)
    tied = lax.optimization_barrier((*by_x, *products(rest_y)))
    by_x = tied[:4]
    parts = exchange_x(tied[4:])
    with jax.named_scope("down"):
        first = down_project(x, by_x, (down_weight, down_other))
    tied = lax.optimization_barrier((*first, *parts))
    first = tied[:4]
    hidden = activate(tied[4:])
    with jax.named_scope("down"):
        second = down_project(x, gather_x(hidden), (down_weight, down_other))
    summed = [sum_y(first), sum_y(second)]
    with jax.named_scope("sum_z"):
        result = summed[0][:local_rows]
        for chunk, total in zip(CHUNKS, summed):
            for place, i in enumerate(chunk):
                if i:
                    block = total[place * local_rows : (place + 1) * local_rows].astype(BF16)
                    result = result + shift(block, "z", i if i <= 4 else i - 8).astype(F32)
    live = live_rows(counts, starts, local_rows)
    return jnp.where(live[:, None], result, 0.0).astype(BF16)


def solution(mesh):
    fine = Mesh(mesh.devices.reshape(2, 4, 8, 2, 2), ("attn", "wa", "z", "yl", "core"))
    rows = ("attn", "z", "yl", "core")
    placed = (P(rows, "wa"), P(), P(), P("wa", rows), P("wa", rows), P(rows, "wa"))
    return jax.shard_map(on_device, mesh=fine, in_specs=placed, out_specs=P(rows, "wa"), check_vma=False)
```

```python
import functools

import jax
import jax.numpy as jnp
from jax import lax
from jax.experimental import pallas as pl
from jax.experimental.pallas import tpu as pltpu
from jax.sharding import Mesh, PartitionSpec as P

GROUPS = 4
CAP = 256
Y = ("attn", "yl")
SIZE = {"z": 8, Y: 4, "wa": 4, "core": 2}
BF16 = jnp.bfloat16
F32 = jnp.float32
CHUNKS = ((0, 1, 7, 4), (2, 3, 6, 5))
DOWN_TILE = 2048
VMEM = 44 * 1024 * 1024


def shift(value, axis, by):
    size = SIZE[axis]
    return lax.ppermute(value, axis, [(i, (i + by) % size) for i in range(size)])


def dot(a, b):
    return jnp.dot(a, b, preferred_element_type=F32)


def gate_up_kernel(x_ref, p0, p1, p2, q2, p3, w0, w1, w2, w3, o0, o1, o2, o3, lhs, held, sems, row_sems):
    rows = p0.shape[0]
    half = held.shape[1] // 2
    copies = [
        [
            pltpu.make_async_copy(
                w.at[pl.ds(part * half, half)], held.at[k, pl.ds(part * half, half)], sems.at[2 * k + part]
            )
            for part in range(2)
        ]
        for k, w in enumerate((w0, w1, w2, w3))
    ]
    into = []
    for i, (j, p) in enumerate(((0, p0), (1, p1), (2, p2), (2, q2), (3, p3))):
        place = lax.rem(4 + j - x_ref[0], 4) * rows + (rows // 2 if i == 3 else 0)
        place = pl.multiple_of(place, rows // 2)
        into.append(pltpu.make_async_copy(p, lhs.at[pl.ds(place, p.shape[0])], row_sems.at[i]))
        into[i].start()
    for copy in copies[0] + copies[1]:
        copy.start()
    for copy in into:
        copy.wait()
    for k in range(4):
        for copy in copies[k]:
            copy.wait()
        if k + 2 < 4:
            for copy in copies[k + 2]:
                copy.start()
        part = dot(lhs[...], held[k])
        for d, o in enumerate((o0, o1, o2, o3)):
            o[k] = part[d * rows : (d + 1) * rows].astype(o.dtype)


def gate_up(x, by_y, weights):
    rows, depth = by_y[0].shape
    width = weights[0].shape[1]
    whole = pl.BlockSpec(memory_space=pltpu.VMEM)
    return pl.pallas_call(
        gate_up_kernel,
        out_shape=[jax.ShapeDtypeStruct((4, rows, width), F32 if d == 0 else BF16) for d in range(4)],
        in_specs=[pl.BlockSpec(memory_space=pltpu.SMEM)] + [pl.BlockSpec(memory_space=pl.ANY)] * 9,
        out_specs=[whole] * 4,
        scratch_shapes=[
            pltpu.VMEM((4 * rows, depth), BF16),
            pltpu.VMEM((4, depth, width), BF16),
            pltpu.SemaphoreType.DMA((8,)),
            pltpu.SemaphoreType.DMA((5,)),
        ],
        compiler_params=pltpu.CompilerParams(vmem_limit_bytes=VMEM),
        cost_estimate=pl.CostEstimate(flops=1, bytes_accessed=1, transcendentals=0),
        name="gate_up",
    )(x, *by_y, *weights)


def down_kernel(x_ref, h0, h1, h2, h3, down, down_other, o0, o1, o2, o3, lhs):
    rows, width = h0.shape[1:]

    @pl.when(pl.program_id(0) == 0)
    def _():
        for d, h in enumerate((h0, h1, h2, h3)):
            place = pl.multiple_of(lax.rem(x_ref[0] + d, 4) * rows, rows)
            lhs[pl.ds(place, rows), :width] = h[0]
            lhs[pl.ds(place, rows), width:] = h[1]

    total = dot(lhs[...], jnp.concatenate([down[...], down_other[...]], axis=0))
    for j, o in enumerate((o0, o1, o2, o3)):
        o[...] = total[j * rows : (j + 1) * rows].astype(o.dtype)


def down_project(x, by_x, weights):
    _, rows, width = by_x[0].shape
    columns = weights[0].shape[1]
    out = pl.BlockSpec((rows, DOWN_TILE), lambda n, x_ref: (0, n))
    return pl.pallas_call(
        down_kernel,
        out_shape=[jax.ShapeDtypeStruct((rows, columns), F32 if j == 0 else BF16) for j in range(4)],
        grid_spec=pltpu.PrefetchScalarGridSpec(
            num_scalar_prefetch=1,
            grid=(columns // DOWN_TILE,),
            in_specs=[pl.BlockSpec((2, rows, width), lambda n, x_ref: (0, 0, 0))] * 4
            + [pl.BlockSpec((width, DOWN_TILE), lambda n, x_ref: (0, n))] * 2,
            out_specs=[out] * 4,
            scratch_shapes=[pltpu.VMEM((4 * rows, 2 * width), BF16)],
        ),
        compiler_params=pltpu.CompilerParams(vmem_limit_bytes=VMEM),
        cost_estimate=pl.CostEstimate(
            flops=2 * 4 * rows * 2 * width * columns, bytes_accessed=4 * width * columns, transcendentals=0
        ),
        name="down",
    )(x, *by_x, *weights)


def gather_y(mine):
    half = mine.shape[0] // 2
    after = shift(mine, Y, -1)
    before = shift(mine, Y, 1)
    return [mine, after, shift(after[:half], Y, -1), shift(before[half:], Y, 1), before]


def live_rows(counts, starts, local_rows):
    first_row = lax.axis_index(("attn", "z", "yl", "core")) * local_rows
    row_ids = first_row + jnp.arange(local_rows, dtype=jnp.int32)
    group = row_ids // CAP
    slot = row_ids % CAP
    onehot = (group[:, None] == jnp.arange(GROUPS, dtype=jnp.int32)[None, :]).astype(jnp.int32)
    start_row = jnp.sum(onehot * starts[None, :], axis=1)
    live_count = jnp.sum(onehot * counts[None, :], axis=1)
    return (slot >= start_row) & (slot < start_row + live_count)


def on_device(tokens, counts, starts, gate_weight, up_weight, down_weight):
    local_rows = tokens.shape[0]
    x = lax.axis_index("wa").astype(jnp.int32).reshape(1)
    with jax.named_scope("swap_weights"):
        gate_other = shift(gate_weight, "core", 1)
        up_other = shift(up_weight, "core", 1)
    with jax.named_scope("gather_z"):
        after = shift(tokens, "z", -1)
        before = shift(tokens, "z", 1)
        far = shift(tokens, "z", 4)
        after, before, far, gate_other, up_other = lax.optimization_barrier(
            (after, before, far, gate_other, up_other)
        )
        near = jnp.concatenate([tokens, after, before, far], axis=0)
        afters = shift(jnp.concatenate([tokens, after], axis=0), "z", -2)
        befores = shift(jnp.concatenate([tokens, before], axis=0), "z", 2)
        rest = jnp.concatenate([afters, befores], axis=0)
    with jax.named_scope("gather_y"):
        near_y = gather_y(near)
        *near_y, rest = lax.optimization_barrier((*near_y, rest))
        rest_y = gather_y(rest)

    def products(by_y):
        with jax.named_scope("gate_up"):
            return gate_up(x, by_y, (gate_weight, gate_other, up_weight, up_other))

    def exchange_x(parts):
        with jax.named_scope("sum_x"):
            return [parts[0], shift(parts[1], "wa", 1), shift(parts[3], "wa", -1), shift(parts[2], "wa", 2)]

    def activate(parts):
        with jax.named_scope("sum_x"):
            total = parts[0]
            for part in parts[1:]:
                total = total + part.astype(F32)
            return (jax.nn.silu(total[:2]) * total[2:]).astype(BF16)

    def gather_x(hidden):
        with jax.named_scope("gather_x"):
            return [hidden, shift(hidden, "wa", -1), shift(hidden, "wa", 2), shift(hidden, "wa", 1)]

    def sum_y(parts):
        with jax.named_scope("sum_y"):
            total = parts[0]
            for q, by in ((parts[1], 1), (parts[3], -1), (parts[2], 2)):
                total = total + shift(q, Y, by).astype(F32)
            return total

    near_y[0], down_tied = lax.optimization_barrier((near_y[0], down_weight))
    with jax.named_scope("swap_down"):
        down_other = shift(down_tied, "core", 1)
    hidden = activate(exchange_x(products(near_y)))
    hidden, down_other, *rest_y = lax.optimization_barrier((hidden, down_other, *rest_y))
    rest_parts = products(rest_y)
    by_x = gather_x(hidden)
    parts = exchange_x(rest_parts)
    with jax.named_scope("down"):
        first = down_project(x, by_x, (down_weight, down_other))
    tied = lax.optimization_barrier((*first, *parts))
    first = tied[:4]
    hidden = activate(tied[4:])
    with jax.named_scope("down"):
        second = down_project(x, gather_x(hidden), (down_weight, down_other))
    summed = [sum_y(first), sum_y(second)]
    with jax.named_scope("sum_z"):
        result = summed[0][:local_rows]
        for chunk, total in zip(CHUNKS, summed):
            for place, i in enumerate(chunk):
                if i:
                    block = total[place * local_rows : (place + 1) * local_rows].astype(BF16)
                    result = result + shift(block, "z", i if i <= 4 else i - 8).astype(F32)
    live = live_rows(counts, starts, local_rows)
    return jnp.where(live[:, None], result, 0.0).astype(BF16)


def solution(mesh):
    fine = Mesh(mesh.devices.reshape(2, 4, 8, 2, 2), ("attn", "wa", "z", "yl", "core"))
    rows = ("attn", "z", "yl", "core")
    placed = (P(rows, "wa"), P(), P(), P("wa", rows), P("wa", rows), P(rows, "wa"))
    return jax.shard_map(on_device, mesh=fine, in_specs=placed, out_specs=P(rows, "wa"), check_vma=False)
```

```python
import functools

import jax
import jax.numpy as jnp
from jax import lax
from jax.experimental import pallas as pl
from jax.experimental.pallas import tpu as pltpu
from jax.sharding import Mesh, PartitionSpec as P

GROUPS = 4
CAP = 256
SENDS = (4, 1, 7, 3, 6, 2, 5)
Y = ("attn", "yl")
SIZE = {"z": 8, Y: 4, "wa": 4, "core": 2}
BF16 = jnp.bfloat16
F32 = jnp.float32
CHUNKS = ((0, 1, 7, 4), (2, 3, 6, 5))
DOWN_TILE = 2048
VMEM = 50 * 1024 * 1024


def shift(value, axis, by):
    size = SIZE[axis]
    return lax.ppermute(value, axis, [(i, (i + by) % size) for i in range(size)])


def dot(a, b):
    return jnp.dot(a, b, preferred_element_type=F32)


def gate_up_kernel(x_ref, p0, p1, p2, q2, p3, w0, w1, w2, w3, o0, o1, o2, o3, lhs, held, sems, row_sems):
    rows = p0.shape[0]
    half = held.shape[1] // 2
    copies = [
        [
            pltpu.make_async_copy(
                w.at[pl.ds(part * half, half)], held.at[k, pl.ds(part * half, half)], sems.at[2 * k + part]
            )
            for part in range(2)
        ]
        for k, w in enumerate((w0, w1, w2, w3))
    ]
    into = []
    for i, (j, p) in enumerate(((0, p0), (1, p1), (2, p2), (2, q2), (3, p3))):
        place = lax.rem(4 + j - x_ref[0], 4) * rows + (rows // 2 if i == 3 else 0)
        place = pl.multiple_of(place, rows // 2)
        into.append(pltpu.make_async_copy(p, lhs.at[pl.ds(place, p.shape[0])], row_sems.at[i]))
        into[i].start()
    for copy in copies[0] + copies[1]:
        copy.start()
    for copy in into:
        copy.wait()
    for k in range(4):
        for copy in copies[k]:
            copy.wait()
        if k + 2 < 4:
            for copy in copies[k + 2]:
                copy.start()
        part = dot(lhs[...], held[k])
        for d, o in enumerate((o0, o1, o2, o3)):
            o[k] = part[d * rows : (d + 1) * rows].astype(o.dtype)


def gate_up(x, by_y, weights):
    rows, depth = by_y[0].shape
    width = weights[0].shape[1]
    whole = pl.BlockSpec(memory_space=pltpu.VMEM)
    return pl.pallas_call(
        gate_up_kernel,
        out_shape=[jax.ShapeDtypeStruct((4, rows, width), F32 if d == 0 else BF16) for d in range(4)],
        in_specs=[pl.BlockSpec(memory_space=pltpu.SMEM)] + [pl.BlockSpec(memory_space=pl.ANY)] * 9,
        out_specs=[whole] * 4,
        scratch_shapes=[
            pltpu.VMEM((4 * rows, depth), BF16),
            pltpu.VMEM((4, depth, width), BF16),
            pltpu.SemaphoreType.DMA((8,)),
            pltpu.SemaphoreType.DMA((5,)),
        ],
        compiler_params=pltpu.CompilerParams(vmem_limit_bytes=VMEM),
        cost_estimate=pl.CostEstimate(flops=1, bytes_accessed=1, transcendentals=0),
        name="gate_up",
    )(x, *by_y, *weights)


def down_kernel(x_ref, h0, h1, h2, h3, down, down_other, o0, o1, o2, o3, lhs):
    rows, width = h0.shape[1:]

    @pl.when(pl.program_id(0) == 0)
    def _():
        for d, h in enumerate((h0, h1, h2, h3)):
            place = pl.multiple_of(lax.rem(x_ref[0] + d, 4) * rows, rows)
            lhs[pl.ds(place, rows), :width] = h[0]
            lhs[pl.ds(place, rows), width:] = h[1]

    total = dot(lhs[...], jnp.concatenate([down[...], down_other[...]], axis=0))
    for j, o in enumerate((o0, o1, o2, o3)):
        o[...] = total[j * rows : (j + 1) * rows].astype(o.dtype)


def down_project(x, by_x, weights):
    _, rows, width = by_x[0].shape
    columns = weights[0].shape[1]
    out = pl.BlockSpec((rows, DOWN_TILE), lambda n, x_ref: (0, n))
    return pl.pallas_call(
        down_kernel,
        out_shape=[jax.ShapeDtypeStruct((rows, columns), F32 if j == 0 else BF16) for j in range(4)],
        grid_spec=pltpu.PrefetchScalarGridSpec(
            num_scalar_prefetch=1,
            grid=(columns // DOWN_TILE,),
            in_specs=[pl.BlockSpec((2, rows, width), lambda n, x_ref: (0, 0, 0))] * 4
            + [pl.BlockSpec((width, DOWN_TILE), lambda n, x_ref: (0, n))] * 2,
            out_specs=[out] * 4,
            scratch_shapes=[pltpu.VMEM((4 * rows, 2 * width), BF16)],
        ),
        compiler_params=pltpu.CompilerParams(vmem_limit_bytes=VMEM),
        cost_estimate=pl.CostEstimate(
            flops=2 * 4 * rows * 2 * width * columns, bytes_accessed=4 * width * columns, transcendentals=0
        ),
        name="down",
    )(x, *by_x, *weights)


def gather_y(mine):
    half = mine.shape[0] // 2
    after = shift(mine, Y, -1)
    before = shift(mine, Y, 1)
    return [mine, after, shift(after[:half], Y, -1), shift(before[half:], Y, 1), before]


def live_rows(counts, starts, local_rows):
    first_row = lax.axis_index(("attn", "z", "yl", "core")) * local_rows
    row_ids = first_row + jnp.arange(local_rows, dtype=jnp.int32)
    group = row_ids // CAP
    slot = row_ids % CAP
    onehot = (group[:, None] == jnp.arange(GROUPS, dtype=jnp.int32)[None, :]).astype(jnp.int32)
    start_row = jnp.sum(onehot * starts[None, :], axis=1)
    live_count = jnp.sum(onehot * counts[None, :], axis=1)
    return (slot >= start_row) & (slot < start_row + live_count)


def on_device(tokens, counts, starts, gate_weight, up_weight, down_weight):
    local_rows = tokens.shape[0]
    x = lax.axis_index("wa").astype(jnp.int32).reshape(1)
    with jax.named_scope("swap_weights"):
        gate_other = shift(gate_weight, "core", 1)
        up_other = shift(up_weight, "core", 1)
    with jax.named_scope("gather_z"):
        after = shift(tokens, "z", -1)
        before = shift(tokens, "z", 1)
        far = shift(tokens, "z", 4)
        after, before, far = lax.optimization_barrier((after, before, far))
        near = jnp.concatenate([tokens, after, before, far], axis=0)
        after, before, gate_other, up_other = lax.optimization_barrier((after, before, gate_other, up_other))
        afters = shift(jnp.concatenate([tokens, after], axis=0), "z", -2)
        befores = shift(jnp.concatenate([tokens, before], axis=0), "z", 2)
        rest = jnp.concatenate([afters, befores], axis=0)
    with jax.named_scope("gather_y"):
        near_y = gather_y(near)
        *near_y, rest = lax.optimization_barrier((*near_y, rest))
        rest_y = gather_y(rest)

    def products(by_y):
        with jax.named_scope("gate_up"):
            return gate_up(x, by_y, (gate_weight, gate_other, up_weight, up_other))

    def exchange_x(parts):
        with jax.named_scope("sum_x"):
            return [parts[0], shift(parts[1], "wa", 1), shift(parts[3], "wa", -1), shift(parts[2], "wa", 2)]

    def activate(parts):
        with jax.named_scope("sum_x"):
            total = parts[0]
            for part in parts[1:]:
                total = total + part.astype(F32)
            return (jax.nn.silu(total[:2]) * total[2:]).astype(BF16)

    def gather_x(hidden):
        with jax.named_scope("gather_x"):
            return [hidden, shift(hidden, "wa", -1), shift(hidden, "wa", 2), shift(hidden, "wa", 1)]

    def sum_y(parts):
        with jax.named_scope("sum_y"):
            total = parts[0]
            for q, by in ((parts[1], 1), (parts[3], -1), (parts[2], 2)):
                total = total + shift(q, Y, by).astype(F32)
            return total

    near_y[0], down_tied = lax.optimization_barrier((near_y[0], down_weight))
    with jax.named_scope("swap_down"):
        down_other = shift(down_tied, "core", 1)
    *parts, down_other = lax.optimization_barrier((*products(near_y), down_other))
    hidden = activate(exchange_x(parts))
    hidden, *rest_y = lax.optimization_barrier((hidden, *rest_y))
    rest_parts = products(rest_y)
    by_x = gather_x(hidden)
    parts = exchange_x(rest_parts)
    with jax.named_scope("down"):
        first = down_project(x, by_x, (down_weight, down_other))
    tied = lax.optimization_barrier((*first, *parts))
    first = tied[:4]
    hidden = activate(tied[4:])
    with jax.named_scope("down"):
        second = down_project(x, gather_x(hidden), (down_weight, down_other))
    summed = [sum_y(first), sum_y(second)]
    with jax.named_scope("sum_z"):
        result = summed[0][:local_rows]
        for chunk, total in zip(CHUNKS, summed):
            for i in SENDS:
                if i in chunk:
                    place = chunk.index(i)
                    block = total[place * local_rows : (place + 1) * local_rows].astype(BF16)
                    result = result + shift(block, "z", i if i <= 4 else i - 8).astype(F32)
    live = live_rows(counts, starts, local_rows)
    return jnp.where(live[:, None], result, 0.0).astype(BF16)


def solution(mesh):
    fine = Mesh(mesh.devices.reshape(2, 4, 8, 2, 2), ("attn", "wa", "z", "yl", "core"))
    rows = ("attn", "z", "yl", "core")
    placed = (P(rows, "wa"), P(), P(), P("wa", rows), P("wa", rows), P(rows, "wa"))
    return jax.shard_map(on_device, mesh=fine, in_specs=placed, out_specs=P(rows, "wa"), check_vma=False)
```

```python
import functools

import jax
import jax.numpy as jnp
from jax import lax
from jax.experimental import pallas as pl
from jax.experimental.pallas import tpu as pltpu
from jax.sharding import Mesh, PartitionSpec as P

GROUPS = 4
CAP = 256
SENDS = (4, 1, 7, 3, 5, 2, 6)
Y = ("attn", "yl")
SIZE = {"z": 8, Y: 4, "wa": 4, "core": 2}
BF16 = jnp.bfloat16
F32 = jnp.float32
CHUNKS = ((0, 1, 7, 4), (2, 3, 6, 5))
DOWN_TILE = 2048
VMEM = 58 * 1024 * 1024


def shift(value, axis, by):
    size = SIZE[axis]
    return lax.ppermute(value, axis, [(i, (i + by) % size) for i in range(size)])


def dot(a, b):
    return jnp.dot(a, b, preferred_element_type=F32)


def gate_up_kernel(x_ref, p0, p1, p2, q2, p3, w0, w1, w2, w3, o0, o1, o2, o3, lhs, held, sems, row_sems):
    rows = p0.shape[0]
    half = held.shape[1] // 2
    copies = [
        [
            pltpu.make_async_copy(
                w.at[pl.ds(part * half, half)], held.at[k, pl.ds(part * half, half)], sems.at[2 * k + part]
            )
            for part in range(2)
        ]
        for k, w in enumerate((w0, w1, w2, w3))
    ]
    into = []
    for i, (j, p) in enumerate(((0, p0), (1, p1), (2, p2), (2, q2), (3, p3))):
        place = lax.rem(4 + j - x_ref[0], 4) * rows + (rows // 2 if i == 3 else 0)
        place = pl.multiple_of(place, rows // 2)
        into.append(pltpu.make_async_copy(p, lhs.at[pl.ds(place, p.shape[0])], row_sems.at[i]))
        into[i].start()
    for copy in copies[0] + copies[1]:
        copy.start()
    for copy in into:
        copy.wait()
    for k in range(4):
        for copy in copies[k]:
            copy.wait()
        if k + 2 < 4:
            for copy in copies[k + 2]:
                copy.start()
        part = dot(lhs[...], held[k])
        for d, o in enumerate((o0, o1, o2, o3)):
            o[k] = part[d * rows : (d + 1) * rows].astype(o.dtype)


def gate_up(x, by_y, weights):
    rows, depth = by_y[0].shape
    width = weights[0].shape[1]
    whole = pl.BlockSpec(memory_space=pltpu.VMEM)
    return pl.pallas_call(
        gate_up_kernel,
        out_shape=[jax.ShapeDtypeStruct((4, rows, width), F32 if d == 0 else BF16) for d in range(4)],
        in_specs=[pl.BlockSpec(memory_space=pltpu.SMEM)] + [pl.BlockSpec(memory_space=pl.ANY)] * 9,
        out_specs=[whole] * 4,
        scratch_shapes=[
            pltpu.VMEM((4 * rows, depth), BF16),
            pltpu.VMEM((4, depth, width), BF16),
            pltpu.SemaphoreType.DMA((8,)),
            pltpu.SemaphoreType.DMA((5,)),
        ],
        compiler_params=pltpu.CompilerParams(vmem_limit_bytes=VMEM),
        cost_estimate=pl.CostEstimate(flops=1, bytes_accessed=1, transcendentals=0),
        name="gate_up",
    )(x, *by_y, *weights)


def down_kernel(x_ref, h0, h1, h2, h3, down, down_other, o0, o1, o2, o3, lhs):
    rows, width = h0.shape[1:]

    @pl.when(pl.program_id(0) == 0)
    def _():
        for d, h in enumerate((h0, h1, h2, h3)):
            place = pl.multiple_of(lax.rem(x_ref[0] + d, 4) * rows, rows)
            lhs[pl.ds(place, rows), :width] = h[0]
            lhs[pl.ds(place, rows), width:] = h[1]

    total = dot(lhs[...], jnp.concatenate([down[...], down_other[...]], axis=0))
    for j, o in enumerate((o0, o1, o2, o3)):
        o[...] = total[j * rows : (j + 1) * rows].astype(o.dtype)


def down_project(x, by_x, weights):
    _, rows, width = by_x[0].shape
    columns = weights[0].shape[1]
    out = pl.BlockSpec((rows, DOWN_TILE), lambda n, x_ref: (0, n))
    return pl.pallas_call(
        down_kernel,
        out_shape=[jax.ShapeDtypeStruct((rows, columns), F32 if j == 0 else BF16) for j in range(4)],
        grid_spec=pltpu.PrefetchScalarGridSpec(
            num_scalar_prefetch=1,
            grid=(columns // DOWN_TILE,),
            in_specs=[pl.BlockSpec((2, rows, width), lambda n, x_ref: (0, 0, 0))] * 4
            + [pl.BlockSpec((width, DOWN_TILE), lambda n, x_ref: (0, n))] * 2,
            out_specs=[out] * 4,
            scratch_shapes=[pltpu.VMEM((4 * rows, 2 * width), BF16)],
        ),
        compiler_params=pltpu.CompilerParams(vmem_limit_bytes=VMEM),
        cost_estimate=pl.CostEstimate(
            flops=2 * 4 * rows * 2 * width * columns, bytes_accessed=4 * width * columns, transcendentals=0
        ),
        name="down",
    )(x, *by_x, *weights)


def gather_y(mine):
    half = mine.shape[0] // 2
    after = shift(mine, Y, -1)
    before = shift(mine, Y, 1)
    return [mine, after, shift(after[:half], Y, -1), shift(before[half:], Y, 1), before]


def live_rows(counts, starts, local_rows):
    first_row = lax.axis_index(("attn", "z", "yl", "core")) * local_rows
    row_ids = first_row + jnp.arange(local_rows, dtype=jnp.int32)
    group = row_ids // CAP
    slot = row_ids % CAP
    onehot = (group[:, None] == jnp.arange(GROUPS, dtype=jnp.int32)[None, :]).astype(jnp.int32)
    start_row = jnp.sum(onehot * starts[None, :], axis=1)
    live_count = jnp.sum(onehot * counts[None, :], axis=1)
    return (slot >= start_row) & (slot < start_row + live_count)


def on_device(tokens, counts, starts, gate_weight, up_weight, down_weight):
    local_rows = tokens.shape[0]
    x = lax.axis_index("wa").astype(jnp.int32).reshape(1)
    with jax.named_scope("swap_weights"):
        gate_other = shift(gate_weight, "core", 1)
        up_other = shift(up_weight, "core", 1)
    with jax.named_scope("gather_z"):
        after = shift(tokens, "z", -1)
        before = shift(tokens, "z", 1)
        far = shift(tokens, "z", 4)
        after, before, far = lax.optimization_barrier((after, before, far))
        near = jnp.concatenate([tokens, after, before, far], axis=0)
        after, before, gate_other, up_other = lax.optimization_barrier((after, before, gate_other, up_other))
        afters = shift(jnp.concatenate([tokens, after], axis=0), "z", -2)
        befores = shift(jnp.concatenate([tokens, before], axis=0), "z", 2)
        rest = jnp.concatenate([afters, befores], axis=0)
    with jax.named_scope("gather_y"):
        near_y = gather_y(near)
        *near_y, rest = lax.optimization_barrier((*near_y, rest))
        rest_y = gather_y(rest)

    def products(by_y):
        with jax.named_scope("gate_up"):
            return gate_up(x, by_y, (gate_weight, gate_other, up_weight, up_other))

    def exchange_x(parts):
        with jax.named_scope("sum_x"):
            return [parts[0], shift(parts[1], "wa", 1), shift(parts[3], "wa", -1), shift(parts[2], "wa", 2)]

    def activate(parts):
        with jax.named_scope("sum_x"):
            total = parts[0]
            for part in parts[1:]:
                total = total + part.astype(F32)
            return (jax.nn.silu(total[:2]) * total[2:]).astype(BF16)

    def gather_x(hidden):
        with jax.named_scope("gather_x"):
            return [hidden, shift(hidden, "wa", -1), shift(hidden, "wa", 2), shift(hidden, "wa", 1)]

    def sum_y(parts):
        with jax.named_scope("sum_y"):
            total = parts[0]
            for q, by in ((parts[1], 1), (parts[3], -1), (parts[2], 2)):
                total = total + shift(q, Y, by).astype(F32)
            return total

    near_y[0], down_tied = lax.optimization_barrier((near_y[0], down_weight))
    with jax.named_scope("swap_down"):
        down_other = shift(down_tied, "core", 1)
    *parts, down_other = lax.optimization_barrier((*products(near_y), down_other))
    hidden = activate(exchange_x(parts))
    hidden, *rest_y = lax.optimization_barrier((hidden, *rest_y))
    rest_parts = products(rest_y)
    by_x = gather_x(hidden)
    parts = exchange_x(rest_parts)
    with jax.named_scope("down"):
        first = down_project(x, by_x, (down_weight, down_other))
    tied = lax.optimization_barrier((*first, *parts))
    first = tied[:4]
    hidden = activate(tied[4:])
    with jax.named_scope("down"):
        second = down_project(x, gather_x(hidden), (down_weight, down_other))
    summed = [sum_y(first), sum_y(second)]
    with jax.named_scope("sum_z"):
        result = summed[0][:local_rows]
        for chunk, total in zip(CHUNKS, summed):
            for i in SENDS:
                if i in chunk:
                    place = chunk.index(i)
                    block = total[place * local_rows : (place + 1) * local_rows].astype(BF16)
                    result = result + shift(block, "z", i if i <= 4 else i - 8).astype(F32)
    live = live_rows(counts, starts, local_rows)
    return jnp.where(live[:, None], result, 0.0).astype(BF16)


def solution(mesh):
    fine = Mesh(mesh.devices.reshape(2, 4, 8, 2, 2), ("attn", "wa", "z", "yl", "core"))
    rows = ("attn", "z", "yl", "core")
    placed = (P(rows, "wa"), P(), P(), P("wa", rows), P("wa", rows), P(rows, "wa"))
    return jax.shard_map(on_device, mesh=fine, in_specs=placed, out_specs=P(rows, "wa"), check_vma=False)
```

```python
import functools

import jax
import jax.numpy as jnp
from jax import lax
from jax.experimental import pallas as pl
from jax.experimental.pallas import tpu as pltpu
from jax.sharding import Mesh, PartitionSpec as P

GROUPS = 4
CAP = 256
SENDS = (4, 1, 7, 3, 6, 2, 5)
Y = ("attn", "yl")
SIZE = {"z": 8, Y: 4, "wa": 4, "core": 2}
BF16 = jnp.bfloat16
F32 = jnp.float32
CHUNKS = ((0, 1, 7, 4), (2, 3, 6, 5))
DOWN_TILE = 2048
VMEM = 50 * 1024 * 1024


def shift(value, axis, by):
    size = SIZE[axis]
    return lax.ppermute(value, axis, [(i, (i + by) % size) for i in range(size)])


def dot(a, b):
    return jnp.dot(a, b, preferred_element_type=F32)


def gate_up_kernel(x_ref, p0, p1, p2, q2, p3, w0, w1, w2, w3, o0, o1, o2, o3, lhs, held, sems, row_sems):
    rows = p0.shape[0]
    half = held.shape[1] // 2
    copies = [
        [
            pltpu.make_async_copy(
                w.at[pl.ds(part * half, half)], held.at[k, pl.ds(part * half, half)], sems.at[2 * k + part]
            )
            for part in range(2)
        ]
        for k, w in enumerate((w0, w1, w2, w3))
    ]
    into = []
    for i, (j, p) in enumerate(((0, p0), (1, p1), (2, p2), (2, q2), (3, p3))):
        place = lax.rem(4 + j - x_ref[0], 4) * rows + (rows // 2 if i == 3 else 0)
        place = pl.multiple_of(place, rows // 2)
        into.append(pltpu.make_async_copy(p, lhs.at[pl.ds(place, p.shape[0])], row_sems.at[i]))
        into[i].start()
    for copy in copies[0] + copies[1] + copies[3]:
        copy.start()
    for copy in into:
        copy.wait()
    for k in (1, 3, 0, 2):
        if k == 3:
            for copy in copies[0]:
                copy.wait()
            for copy in copies[2]:
                copy.start()
        if k != 0:
            for copy in copies[k]:
                copy.wait()
        part = dot(lhs[...], held[k])
        for d, o in enumerate((o0, o1, o2, o3)):
            o[k] = part[d * rows : (d + 1) * rows].astype(o.dtype)


def gate_up(x, by_y, weights):
    rows, depth = by_y[0].shape
    width = weights[0].shape[1]
    whole = pl.BlockSpec(memory_space=pltpu.VMEM)
    return pl.pallas_call(
        gate_up_kernel,
        out_shape=[jax.ShapeDtypeStruct((4, rows, width), F32 if d == 0 else BF16) for d in range(4)],
        in_specs=[pl.BlockSpec(memory_space=pltpu.SMEM)] + [pl.BlockSpec(memory_space=pl.ANY)] * 9,
        out_specs=[whole] * 4,
        scratch_shapes=[
            pltpu.VMEM((4 * rows, depth), BF16),
            pltpu.VMEM((4, depth, width), BF16),
            pltpu.SemaphoreType.DMA((8,)),
            pltpu.SemaphoreType.DMA((5,)),
        ],
        compiler_params=pltpu.CompilerParams(vmem_limit_bytes=VMEM),
        cost_estimate=pl.CostEstimate(flops=1, bytes_accessed=1, transcendentals=0),
        name="gate_up",
    )(x, *by_y, *weights)


def down_kernel(x_ref, h0, h1, h2, h3, down, down_other, o0, o1, o2, o3, lhs):
    rows, width = h0.shape[1:]

    @pl.when(pl.program_id(0) == 0)
    def _():
        for d, h in enumerate((h0, h1, h2, h3)):
            place = pl.multiple_of(lax.rem(x_ref[0] + d, 4) * rows, rows)
            lhs[pl.ds(place, rows), :width] = h[0]
            lhs[pl.ds(place, rows), width:] = h[1]

    total = dot(lhs[...], jnp.concatenate([down[...], down_other[...]], axis=0))
    for j, o in enumerate((o0, o1, o2, o3)):
        o[...] = total[j * rows : (j + 1) * rows].astype(o.dtype)


def down_project(x, by_x, weights):
    _, rows, width = by_x[0].shape
    columns = weights[0].shape[1]
    out = pl.BlockSpec((rows, DOWN_TILE), lambda n, x_ref: (0, n))
    return pl.pallas_call(
        down_kernel,
        out_shape=[jax.ShapeDtypeStruct((rows, columns), F32 if j == 0 else BF16) for j in range(4)],
        grid_spec=pltpu.PrefetchScalarGridSpec(
            num_scalar_prefetch=1,
            grid=(columns // DOWN_TILE,),
            in_specs=[pl.BlockSpec((2, rows, width), lambda n, x_ref: (0, 0, 0))] * 4
            + [pl.BlockSpec((width, DOWN_TILE), lambda n, x_ref: (0, n))] * 2,
            out_specs=[out] * 4,
            scratch_shapes=[pltpu.VMEM((4 * rows, 2 * width), BF16)],
        ),
        compiler_params=pltpu.CompilerParams(vmem_limit_bytes=VMEM),
        cost_estimate=pl.CostEstimate(
            flops=2 * 4 * rows * 2 * width * columns, bytes_accessed=4 * width * columns, transcendentals=0
        ),
        name="down",
    )(x, *by_x, *weights)


def gather_y(mine):
    half = mine.shape[0] // 2
    after = shift(mine, Y, -1)
    before = shift(mine, Y, 1)
    return [mine, after, shift(after[:half], Y, -1), shift(before[half:], Y, 1), before]


def live_rows(counts, starts, local_rows):
    first_row = lax.axis_index(("attn", "z", "yl", "core")) * local_rows
    row_ids = first_row + jnp.arange(local_rows, dtype=jnp.int32)
    group = row_ids // CAP
    slot = row_ids % CAP
    onehot = (group[:, None] == jnp.arange(GROUPS, dtype=jnp.int32)[None, :]).astype(jnp.int32)
    start_row = jnp.sum(onehot * starts[None, :], axis=1)
    live_count = jnp.sum(onehot * counts[None, :], axis=1)
    return (slot >= start_row) & (slot < start_row + live_count)


def on_device(tokens, counts, starts, gate_weight, up_weight, down_weight):
    local_rows = tokens.shape[0]
    x = lax.axis_index("wa").astype(jnp.int32).reshape(1)
    with jax.named_scope("swap_weights"):
        gate_other = shift(gate_weight, "core", 1)
        up_other = shift(up_weight, "core", 1)
    with jax.named_scope("gather_z"):
        after = shift(tokens, "z", -1)
        before = shift(tokens, "z", 1)
        far = shift(tokens, "z", 4)
        after, before, far = lax.optimization_barrier((after, before, far))
        near = jnp.concatenate([tokens, after, before, far], axis=0)
        after, before, gate_other, up_other = lax.optimization_barrier((after, before, gate_other, up_other))
        afters = shift(jnp.concatenate([tokens, after], axis=0), "z", -2)
        befores = shift(jnp.concatenate([tokens, before], axis=0), "z", 2)
        rest = jnp.concatenate([afters, befores], axis=0)
    with jax.named_scope("gather_y"):
        near_y = gather_y(near)
        *near_y, rest = lax.optimization_barrier((*near_y, rest))
        rest_y = gather_y(rest)

    def products(by_y):
        with jax.named_scope("gate_up"):
            return gate_up(x, by_y, (gate_weight, gate_other, up_weight, up_other))

    def exchange_x(parts):
        with jax.named_scope("sum_x"):
            return [parts[0], shift(parts[1], "wa", 1), shift(parts[3], "wa", -1), shift(parts[2], "wa", 2)]

    def activate(parts):
        with jax.named_scope("sum_x"):
            total = parts[0]
            for part in parts[1:]:
                total = total + part.astype(F32)
            return (jax.nn.silu(total[:2]) * total[2:]).astype(BF16)

    def gather_x(hidden):
        with jax.named_scope("gather_x"):
            return [hidden, shift(hidden, "wa", -1), shift(hidden, "wa", 2), shift(hidden, "wa", 1)]

    def sum_y(parts):
        with jax.named_scope("sum_y"):
            total = parts[0]
            for q, by in ((parts[1], 1), (parts[3], -1), (parts[2], 2)):
                total = total + shift(q, Y, by).astype(F32)
            return total

    near_y[0], down_tied = lax.optimization_barrier((near_y[0], down_weight))
    with jax.named_scope("swap_down"):
        down_other = shift(down_tied, "core", 1)
    *parts, down_other = lax.optimization_barrier((*products(near_y), down_other))
    hidden = activate(exchange_x(parts))
    hidden, *rest_y = lax.optimization_barrier((hidden, *rest_y))
    rest_parts = products(rest_y)
    by_x = gather_x(hidden)
    parts = exchange_x(rest_parts)
    with jax.named_scope("down"):
        first = down_project(x, by_x, (down_weight, down_other))
    tied = lax.optimization_barrier((*first, *parts))
    first = tied[:4]
    hidden = activate(tied[4:])
    with jax.named_scope("down"):
        second = down_project(x, gather_x(hidden), (down_weight, down_other))
    summed = [sum_y(first), sum_y(second)]
    with jax.named_scope("sum_z"):
        result = summed[0][:local_rows]
        for chunk, total in zip(CHUNKS, summed):
            for i in SENDS:
                if i in chunk:
                    place = chunk.index(i)
                    block = total[place * local_rows : (place + 1) * local_rows].astype(BF16)
                    result = result + shift(block, "z", i if i <= 4 else i - 8).astype(F32)
    live = live_rows(counts, starts, local_rows)
    return jnp.where(live[:, None], result, 0.0).astype(BF16)


def solution(mesh):
    fine = Mesh(mesh.devices.reshape(2, 4, 8, 2, 2), ("attn", "wa", "z", "yl", "core"))
    rows = ("attn", "z", "yl", "core")
    placed = (P(rows, "wa"), P(), P(), P("wa", rows), P("wa", rows), P(rows, "wa"))
    return jax.shard_map(on_device, mesh=fine, in_specs=placed, out_specs=P(rows, "wa"), check_vma=False)
```
